32 devices in a mesh: rows: 8 (over z, x), delay: 4 (over y, core).
Axes of the slice: x: 2, y: 2, z: 4, core: 2. Of those that a mesh axis runs over, the one named last changes fastest.
Arguments:
- excitation: bfloat16 [4, 80, 16384], P(None, None, 'rows'), may hold values from -6 to 6
- past_currents: bfloat16 [4, 80, 16384], P('delay', None, 'rows'), may hold values from -6 to 6
- history_mats: bfloat16 [4, 16384, 16384], P('delay', 'rows'), may hold values from -0.0234375 to 0.0234375
- inverse: bfloat16 [16384, 16384], P('delay', 'rows'), may hold values from -0.046875 to 0.046875
Outputs:
- currents: float32 [4, 80, 16384], P(None, None, ('delay', 'rows'))
The draws below stay inside these ranges and needn't reach their ends.
All inputs are finite; a program needn't handle non-finite values.
Results may differ from the reference program's by a relative error of at most 0.02.
Values may be sent and summed in bfloat16 or wider, within the bound.
A program may use at most 192 MiB of HBM per device.

```python
import jax
import jax.numpy as jnp

N = 16384
EXC = 80
STEPS = 4
DELAYS = 4


def shard_levels(rng, shape, pieces, smallest, high):
    factor_of, own = 1.0, jax.random.fold_in(rng, 6)
    for dim, shards_of in pieces:
        steps = jnp.exp(jax.random.uniform(jax.random.fold_in(own, dim), (shards_of,), jnp.float32, smallest / len(pieces), high / len(pieces)))
        factor_of = factor_of * jnp.repeat(steps, shape[dim] // shards_of).reshape([-1 if axis == dim else 1 for axis in range(len(shape))])
    return factor_of


def noise(key, extent, spread, reach, cuts=(), kind=jnp.bfloat16):
    factor_of = shard_levels(key, extent, cuts, -0.22, 0.18) if cuts else 1.0
    drawn = jax.random.normal(key, extent, jnp.float32) * spread * factor_of
    return jnp.minimum(jnp.maximum(drawn, -reach), reach).astype(kind)


def setup_inputs(seed: int = 0) -> dict:
    key_of = jax.random.split(jax.random.key(seed), 5)
    excitation = noise(key_of[0], (STEPS, EXC, N), 1.0, 6.0, ((2, 8),))
    past_currents = noise(key_of[1], (DELAYS, EXC, N), 1.0, 6.0, ((0, 4), (2, 8)))
    history_mats = noise(key_of[2], (DELAYS, N, N), (DELAYS * N) ** -0.5, 0.0234375, ((0, 4), (1, 8)))
    inverse = noise(key_of[3], (N, N), N ** -0.5, 0.046875, ((0, 4), (1, 8)))
    return {"excitation": excitation, "past_currents": past_currents, "history_mats": history_mats, "inverse": inverse}


def reference(excitation, past_currents, history_mats, inverse):
    recent = [past_currents[lag_index] for lag_index in range(DELAYS)]
    results = []
    for step in range(STEPS):
        history = jnp.zeros((EXC, N), jnp.float32)
        for lag_index in range(DELAYS):
            history = history + jnp.dot(recent[lag_index], history_mats[lag_index].T, preferred_element_type=jnp.float32)
        drive_rows = (excitation[step].astype(jnp.float32) - history).astype(jnp.bfloat16)
        current = jnp.dot(drive_rows, inverse.T, preferred_element_type=jnp.float32)
        results.append(current)
        recent = [current.astype(jnp.bfloat16)] + recent[:-1]
    return jnp.stack(results)
```

```python
import functools

import jax
import jax.numpy as jnp
from jax import lax
from jax.experimental import pallas as pl
from jax.experimental.pallas import tpu as pltpu
from jax.sharding import PartitionSpec as P


def on_device(excitation, past_currents, history_mats, inverse):
    delay_count = lax.axis_size("delay")
    delay_pos = lax.axis_index("delay")
    steps_total = excitation.shape[0]
    local_mat = history_mats[0]
    all_past = lax.all_gather(past_currents, "delay", axis=0, tiled=True)
    all_past = lax.all_gather(all_past, "rows", axis=2, tiled=True)
    window = all_past[::-1]
    delayed_cur = lax.dynamic_index_in_dim(window, delay_count - 1 - delay_pos, 0, keepdims=False)
    results = []
    for step in range(steps_total):
        partial_hist = jnp.dot(delayed_cur, local_mat.T, preferred_element_type=jnp.float32)
        history = lax.psum(partial_hist.astype(jnp.bfloat16), "delay").astype(jnp.float32)
        drive_rows = (excitation[step].astype(jnp.float32) - history).astype(jnp.bfloat16)
        products = lax.dot_general(
            drive_rows, inverse, (((1,), (1,)), ((), ())), preferred_element_type=jnp.float32
        )
        own_piece = lax.psum_scatter(products, "rows", scatter_dimension=1, tiled=True)
        if step + 1 < steps_total:
            group_part = lax.all_gather(own_piece.astype(jnp.bfloat16), "rows", axis=1, tiled=True)
        results.append(own_piece)
        if step + 1 < steps_total:
            newest = lax.all_gather(group_part, "delay", axis=1, tiled=True)
            window = jnp.concatenate([window[1:], newest[None]], axis=0)
            delayed_cur = lax.dynamic_index_in_dim(
                window, delay_count - 1 - delay_pos, 0, keepdims=False
            )
    return jnp.stack(results)


MESH = pl.DeviceIdType.MESH
F32, BF16 = jnp.float32, jnp.bfloat16
SLOTS = 12


def dot_rows(a, b):
    return lax.dot_general(a, b, (((1,), (1,)), ((), ())), preferred_element_type=F32)


def march(R, D, S, exc, past, mats, inv_hbm, out, xs, hbuf, inv, total, parts, part_out, drive,
          red_out, red_in, newest, hsem, inv_sem, blk_send, blk_recv, blk_fwd, pc_send, pc_recv,
          pc_fwd, sh_send, sh_recv, part_send, part_recv, drv_send, drv_recv, red_send, red_recv):
    r, d = lax.axis_index("rows"), lax.axis_index("delay")
    Z, NP = R // 2, R * D
    E, W = total.shape
    P = W // D
    z, x = r // 2, lax.rem(r, 2)
    mate = r + 1 - 2 * x
    half = W // 4

    def lane(o):
        return lax.rem(z + o, Z) * 2 + x

    def source(o):
        return lax.rem(z + o, Z) * 2 + jnp.where(o < Z, x, 1 - x)

    def remote(src, dst, send, recv, row, delay):
        return pltpu.make_async_remote_copy(
            src_ref=src, dst_ref=dst, send_sem=send, recv_sem=recv,
            device_id={"rows": row, "delay": delay}, device_id_type=MESH)

    def chunk_copy(t):
        s, k = t // NP, lax.rem(t, NP)
        src, e = source(k // D), lax.rem(k, D)
        q = jnp.where(s == 0, src * D + e, e * R + src)
        slot = lax.rem(t, SLOTS)
        return pltpu.make_async_copy(
            mats.at[:, pl.ds(pl.multiple_of(q * P, P), P)], hbuf.at[slot], hsem.at[slot])

    def prefetch(t, c):
        chunk_copy(t).start()
        return c

    lax.fori_loop(0, SLOTS, prefetch, 0)
    inv_copy = pltpu.make_async_copy(inv_hbm, inv, inv_sem)
    inv_copy.start()

    barrier = pltpu.get_barrier_semaphore()

    def greet(row, delay):
        pl.semaphore_signal(barrier, inc=1, device_id={"rows": row, "delay": delay}, device_id_type=MESH)

    for o in range(1, R):
        greet(lax.rem(r + o, R), d)
    for o in range(1, D):
        greet(r, lax.rem(d + o, D))

    @pl.when(d == 0)
    def _():
        for o in range(1, Z):
            for e in range(1, D):
                greet(lane(o), e)
        pl.semaphore_wait(barrier, R - 1 + D - 1 + (Z - 1) * (D - 1))

    @pl.when(d != 0)
    def _():
        for o in range(1, Z):
            greet(lane(o), 0)
        pl.semaphore_wait(barrier, R - 1 + D - 1 + Z - 1)

    def block(row):
        return xs.at[0, pl.ds(row * D, D)]

    def multiply(s, k, q):
        t = s * NP + k
        slot = lax.rem(t, SLOTS)
        chunk_copy(t).wait()
        piece = xs[s, q]
        for i in range(4):
            at = pl.ds(i * half, half)
            total[:, at] += dot_rows(piece, hbuf[slot, at, :])

        @pl.when(t + SLOTS < S * NP)
        def _():
            chunk_copy(t + SLOTS).start()

    for e in range(D):
        xs[0, r * D + e] = past[:, e * P:(e + 1) * P]
    for o in range(1, Z):
        remote(block(r), block(r), blk_send.at[o - 1], blk_recv.at[r], lane(o), d).start()

    for s in range(S):
        total[...] = jnp.zeros_like(total)
        if s == 0:
            def by_block(o, c):
                src = source(o)

                @pl.when(o != 0)
                def _():
                    remote(block(src), block(src), blk_fwd.at[0], blk_recv.at[src], mate, d).wait_recv()

                @pl.when(o < Z)
                def _():
                    remote(block(src), block(src), blk_fwd.at[o], blk_recv.at[src], mate, d).start()

                def by_piece(e, c):
                    multiply(0, o * D + e, src * D + e)
                    return c

                return lax.fori_loop(0, D, by_piece, c)

            lax.fori_loop(0, R, by_block, 0)
            for o in range(1, Z):
                remote(block(r), block(r), blk_send.at[o - 1], blk_recv.at[r], lane(o), d).wait_send()
            for o in range(Z):
                remote(block(r), block(r), blk_fwd.at[o], blk_recv.at[r], mate, d).wait_send()
        else:
            @pl.when(d != 0)
            def _():
                remote(xs.at[s - 1], xs.at[s], sh_send.at[s - 1], sh_recv.at[s - 1], r, d - 1).wait_recv()

            if s < S - 1:
                @pl.when(jnp.logical_and(d != 0, d < D - 1))
                def _():
                    remote(xs.at[s], xs.at[s + 1], sh_send.at[s], sh_recv.at[s], r, d + 1).start()

            def by_piece(k, c):
                o, e = k // D, lax.rem(k, D)
                q = e * R + source(o)
                piece = xs.at[s, q]

                @pl.when(jnp.logical_and(d == 0, k != 0))
                def _():
                    remote(piece, piece, pc_fwd.at[0], pc_recv.at[s - 1, q], mate, 0).wait_recv()

                @pl.when(jnp.logical_and(d == 0, o < Z))
                def _():
                    remote(piece, piece, pc_fwd.at[k], pc_recv.at[s - 1, q], mate, 0).start()

                multiply(s, k, q)
                return c

            lax.fori_loop(0, NP, by_piece, 0)

            @pl.when(d == 0)
            def _():
                def sent(k, c):
                    remote(xs.at[s, 0], xs.at[s, 0], pc_fwd.at[k], pc_recv.at[s - 1, 0], mate, 0).wait_send()
                    return c

                lax.fori_loop(0, Z * D, sent, 0)

        if s < S - 1:
            first = (d == 0) if s > 0 else (d < D - 1)

            @pl.when(first)
            def _():
                remote(xs.at[s], xs.at[s + 1], sh_send.at[s], sh_recv.at[s], r, d + 1).start()

        @pl.when(d != 0)
        def _():
            part_out[...] = total[...].astype(BF16)
            up = remote(part_out, parts.at[d - 1], part_send, part_recv.at[d - 1], r, 0)
            up.start()
            up.wait_send()
            remote(drive, drive, drv_send.at[0], drv_recv, r, 0).wait_recv()

        @pl.when(d == 0)
        def _():
            for e in range(D - 1):
                remote(part_out, parts.at[e], part_send, part_recv.at[e], r, e + 1).wait_recv()
            history = total[...]
            for e in range(D - 1):
                history = history + parts[e].astype(F32)
            drive[...] = (exc[s].astype(F32) - history).astype(BF16)
            downs = [remote(drive, drive, drv_send.at[e - 1], drv_recv, r, e) for e in range(D - 1, 0, -1)]
            for down in downs:
                down.start()

        if s == 0:
            inv_copy.wait()

        def by_row(o, c):
            to = lax.rem(r + o + 1, R)
            red_out[o] = dot_rows(
                drive[...], inv[pl.ds(pl.multiple_of(to * P, P), P), :]).astype(BF16)
            remote(red_out.at[o], red_in.at[o], red_send.at[o], red_recv.at[o], to, d).start()
            return c

        lax.fori_loop(0, R - 1, by_row, 0)
        current = dot_rows(drive[...], inv[pl.ds(pl.multiple_of(r * P, P), P), :])
        for o in range(R - 1):
            remote(red_out.at[o], red_in.at[o], red_send.at[o], red_recv.at[o], r, d).wait()
            current = current + red_in[o].astype(F32)
        out[s] = current

        @pl.when(d == 0)
        def _():
            for e in range(D - 1, 0, -1):
                remote(drive, drive, drv_send.at[e - 1], drv_recv, r, e).wait_send()

        if s < S - 1:
            mine = d * R + r
            newest[s] = current.astype(BF16)
            for o in list(range(1, Z)) + [0]:
                send = remote(newest.at[s], xs.at[s + 1, mine], pc_send.at[s, o],
                              pc_recv.at[s, mine], lane(o), 0)
                if o == 0:
                    pl.when(d != 0)(send.start)
                else:
                    send.start()

            @pl.when(d == 0)
            def _():
                xs[s + 1, mine] = current.astype(BF16)

    for s in range(S - 1):
        for o in range(Z):
            send = remote(newest.at[s], newest.at[s], pc_send.at[s, o], pc_recv.at[s, 0], r, 0)
            if o == 0:
                pl.when(d != 0)(send.wait_send)
            else:
                send.wait_send()

        @pl.when(d < D - 1)
        def _():
            remote(xs.at[s], xs.at[s + 1], sh_send.at[s], sh_recv.at[s], r, d + 1).wait_send()


def in_one_kernel(excitation, past_currents, history_mats, inverse):
    R, D = lax.axis_size("rows"), lax.axis_size("delay")
    S, E, W = excitation.shape
    N, P, Z = W * R, W // D, R // 2
    NP = R * D
    dma = pltpu.SemaphoreType.DMA
    vmem, anywhere = pl.BlockSpec(memory_space=pltpu.VMEM), pl.BlockSpec(memory_space=pl.ANY)
    return pl.pallas_call(
        functools.partial(march, R, D, S),
        out_shape=jax.ShapeDtypeStruct((S, E, P), F32),
        in_specs=[vmem, vmem, anywhere, anywhere],
        out_specs=vmem,
        scratch_shapes=[
            pltpu.VMEM((S, NP, E, P), BF16),
            pltpu.VMEM((SLOTS, W, P), BF16),
            pltpu.VMEM((N // D, W), BF16),
            pltpu.VMEM((E, W), F32),
            pltpu.VMEM((D - 1, E, W), BF16),
            pltpu.VMEM((E, W), BF16),
            pltpu.VMEM((E, W), BF16),
            pltpu.VMEM((R - 1, E, P), BF16),
            pltpu.VMEM((R - 1, E, P), BF16),
            pltpu.VMEM((S - 1, E, P), BF16),
            dma((SLOTS,)), dma(()),
            dma((Z - 1,)), dma((R,)), dma((Z,)),
            dma((S - 1, Z)), dma((S - 1, NP)), dma((Z * D,)),
            dma((S - 1,)), dma((S - 1,)),
            dma(()), dma((D - 1,)),
            dma((D - 1,)), dma(()),
            dma((R - 1,)), dma((R - 1,)),
        ],
        compiler_params=pltpu.CompilerParams(
            collective_id=0, has_side_effects=True, vmem_limit_bytes=62 * 2**20),
        cost_estimate=pl.CostEstimate(
            flops=2 * S * E * (N * W + N // D * W), bytes_accessed=2 * S * N * W, transcendentals=0),
    )(excitation, past_currents[0], history_mats[0], inverse)


def solution(mesh):
    in_specs = (
        P(None, None, "rows"),
        P("delay", None, "rows"),
        P("delay", "rows", None),
        P("delay", "rows"),
    )
    out_specs = P(None, None, ("delay", "rows"))
    rows, delays = mesh.shape["rows"], mesh.shape["delay"]

    def body(excitation, past_currents, history_mats, inverse):
        steps, _, width = excitation.shape
        fits = width % (delays * 128) == 0 and rows % 2 == 0 and rows <= 8
        run = in_one_kernel if fits else on_device
        return run(excitation, past_currents, history_mats, inverse)

    return jax.shard_map(
        body, mesh=mesh, in_specs=in_specs, out_specs=out_specs, check_vma=False
    )
```

```python
import functools

import jax
import jax.numpy as jnp
from jax import lax
from jax.experimental import pallas as pl
from jax.experimental.pallas import tpu as pltpu
from jax.sharding import PartitionSpec as P


def on_device(excitation, past_currents, history_mats, inverse):
    delay_count = lax.axis_size("delay")
    delay_pos = lax.axis_index("delay")
    steps_total = excitation.shape[0]
    local_mat = history_mats[0]
    all_past = lax.all_gather(past_currents, "delay", axis=0, tiled=True)
    all_past = lax.all_gather(all_past, "rows", axis=2, tiled=True)
    window = all_past[::-1]
    delayed_cur = lax.dynamic_index_in_dim(window, delay_count - 1 - delay_pos, 0, keepdims=False)
    results = []
    for step in range(steps_total):
        partial_hist = jnp.dot(delayed_cur, local_mat.T, preferred_element_type=jnp.float32)
        history = lax.psum(partial_hist.astype(jnp.bfloat16), "delay").astype(jnp.float32)
        drive_rows = (excitation[step].astype(jnp.float32) - history).astype(jnp.bfloat16)
        products = lax.dot_general(
            drive_rows, inverse, (((1,), (1,)), ((), ())), preferred_element_type=jnp.float32
        )
        own_piece = lax.psum_scatter(products, "rows", scatter_dimension=1, tiled=True)
        if step + 1 < steps_total:
            group_part = lax.all_gather(own_piece.astype(jnp.bfloat16), "rows", axis=1, tiled=True)
        results.append(own_piece)
        if step + 1 < steps_total:
            newest = lax.all_gather(group_part, "delay", axis=1, tiled=True)
            window = jnp.concatenate([window[1:], newest[None]], axis=0)
            delayed_cur = lax.dynamic_index_in_dim(
                window, delay_count - 1 - delay_pos, 0, keepdims=False
            )
    return jnp.stack(results)


MESH = pl.DeviceIdType.MESH
F32, BF16 = jnp.float32, jnp.bfloat16
SLOTS = 12


def dot_rows(a, b):
    return lax.dot_general(a, b, (((1,), (1,)), ((), ())), preferred_element_type=F32)


def march(R, D, S, exc, past, mats, inv_hbm, out, xs, hbuf, inv, total, parts, part_out, drive,
          red_out, red_in, newest, hsem, inv_sem, blk_send, blk_recv, blk_fwd, pc_send, pc_recv,
          pc_fwd, sh_send, sh_recv, shb_send, shb_recv, part_send, part_recv, drv_send, drv_recv, red_send, red_recv):
    r, d = lax.axis_index("rows"), lax.axis_index("delay")
    Z, NP = R // 2, R * D
    E, W = total.shape
    P = W // D
    z, x = r // 2, lax.rem(r, 2)
    mate = r + 1 - 2 * x
    half = W // 4

    def lane(o):
        return lax.rem(z + o, Z) * 2 + x

    def source(o):
        return lax.rem(z + o, Z) * 2 + jnp.where(o < Z, x, 1 - x)

    def remote(src, dst, send, recv, row, delay):
        return pltpu.make_async_remote_copy(
            src_ref=src, dst_ref=dst, send_sem=send, recv_sem=recv,
            device_id={"rows": row, "delay": delay}, device_id_type=MESH)

    def chunk_copy(t):
        s, k = t // NP, lax.rem(t, NP)
        src, e = source(k // D), lax.rem(k, D)
        q = jnp.where(s == 0, src * D + e, e * R + src)
        slot = lax.rem(t, SLOTS)
        return pltpu.make_async_copy(
            mats.at[:, pl.ds(pl.multiple_of(q * P, P), P)], hbuf.at[slot], hsem.at[slot])

    def prefetch(t, c):
        chunk_copy(t).start()
        return c

    lax.fori_loop(0, SLOTS, prefetch, 0)
    inv_copy = pltpu.make_async_copy(inv_hbm, inv, inv_sem)
    inv_copy.start()

    barrier = pltpu.get_barrier_semaphore()

    def greet(row, delay):
        pl.semaphore_signal(barrier, inc=1, device_id={"rows": row, "delay": delay}, device_id_type=MESH)

    for o in range(1, R):
        greet(lax.rem(r + o, R), d)
    for o in range(1, D):
        greet(r, lax.rem(d + o, D))

    @pl.when(d == 0)
    def _():
        for o in range(1, Z):
            for e in range(1, D):
                greet(lane(o), e)
        pl.semaphore_wait(barrier, R - 1 + D - 1 + (Z - 1) * (D - 1))

    @pl.when(d != 0)
    def _():
        for o in range(1, Z):
            greet(lane(o), 0)
        pl.semaphore_wait(barrier, R - 1 + D - 1 + Z - 1)

    def block(row):
        return xs.at[0, pl.ds(row * D, D)]

    def shift_block(o):
        src = source(o)
        return remote(block(src), xs.at[1, pl.ds(src * D, D)], shb_send.at[o], shb_recv.at[o], r, d + 1)

    def multiply(s, k, q):
        t = s * NP + k
        slot = lax.rem(t, SLOTS)
        chunk_copy(t).wait()
        piece = xs[s, q]
        for i in range(4):
            at = pl.ds(i * half, half)
            total[:, at] += dot_rows(piece, hbuf[slot, at, :])

        @pl.when(t + SLOTS < S * NP)
        def _():
            chunk_copy(t + SLOTS).start()

    for e in range(D):
        xs[0, r * D + e] = past[:, e * P:(e + 1) * P]
    for o in range(1, Z):
        remote(block(r), block(r), blk_send.at[o - 1], blk_recv.at[r], lane(o), d).start()

    for s in range(S):
        total[...] = jnp.zeros_like(total)
        if s == 0:
            def by_block(o, c):
                src = source(o)

                @pl.when(o != 0)
                def _():
                    remote(block(src), block(src), blk_fwd.at[0], blk_recv.at[src], mate, d).wait_recv()

                @pl.when(o < Z)
                def _():
                    remote(block(src), block(src), blk_fwd.at[o], blk_recv.at[src], mate, d).start()

                @pl.when(d < D - 1)
                def _():
                    shift_block(o).start()

                def by_piece(e, c):
                    multiply(0, o * D + e, src * D + e)
                    return c

                return lax.fori_loop(0, D, by_piece, c)

            lax.fori_loop(0, R, by_block, 0)
            for o in range(1, Z):
                remote(block(r), block(r), blk_send.at[o - 1], blk_recv.at[r], lane(o), d).wait_send()
            for o in range(Z):
                remote(block(r), block(r), blk_fwd.at[o], blk_recv.at[r], mate, d).wait_send()
        else:
            @pl.when(d != 0)
            def _():
                if s == 1:
                    for o in range(R):
                        shift_block(o).wait_recv()
                else:
                    remote(xs.at[s - 1], xs.at[s], sh_send.at[s - 1], sh_recv.at[s - 1], r, d - 1).wait_recv()

            if s < S - 1:
                @pl.when(jnp.logical_and(d != 0, d < D - 1))
                def _():
                    remote(xs.at[s], xs.at[s + 1], sh_send.at[s], sh_recv.at[s], r, d + 1).start()

            def by_piece(k, c):
                o, e = k // D, lax.rem(k, D)
                q = e * R + source(o)
                piece = xs.at[s, q]

                @pl.when(jnp.logical_and(d == 0, k != 0))
                def _():
                    remote(piece, piece, pc_fwd.at[0], pc_recv.at[s - 1, q], mate, 0).wait_recv()

                @pl.when(jnp.logical_and(d == 0, o < Z))
                def _():
                    remote(piece, piece, pc_fwd.at[k], pc_recv.at[s - 1, q], mate, 0).start()

                multiply(s, k, q)
                return c

            lax.fori_loop(0, NP, by_piece, 0)

            @pl.when(d == 0)
            def _():
                def sent(k, c):
                    remote(xs.at[s, 0], xs.at[s, 0], pc_fwd.at[k], pc_recv.at[s - 1, 0], mate, 0).wait_send()
                    return c

                lax.fori_loop(0, Z * D, sent, 0)

        @pl.when(d != 0)
        def _():
            part_out[...] = total[...].astype(BF16)
            up = remote(part_out, parts.at[d - 1], part_send, part_recv.at[d - 1], r, 0)
            up.start()
            up.wait_send()
            remote(drive, drive, drv_send.at[0], drv_recv, r, 0).wait_recv()

        @pl.when(d == 2)
        def _():
            remote(drive, drive, drv_send.at[0], drv_recv, r, 3).start()

        @pl.when(d == 0)
        def _():
            for e in range(D - 1):
                remote(part_out, parts.at[e], part_send, part_recv.at[e], r, e + 1).wait_recv()
            history = total[...]
            for e in range(D - 1):
                history = history + parts[e].astype(F32)
            drive[...] = (exc[s].astype(F32) - history).astype(BF16)
            downs = [remote(drive, drive, drv_send.at[e - 1], drv_recv, r, e) for e in (2, 1)]
            for down in downs:
                down.start()

        if s == 0:
            inv_copy.wait()

        def by_row(o, c):
            to = lax.rem(r + o + 1, R)
            red_out[o] = dot_rows(
                drive[...], inv[pl.ds(pl.multiple_of(to * P, P), P), :]).astype(BF16)
            remote(red_out.at[o], red_in.at[o], red_send.at[o], red_recv.at[o], to, d).start()
            return c

        lax.fori_loop(0, R - 1, by_row, 0)
        if 0 < s < S - 1:
            @pl.when(d == 0)
            def _():
                remote(xs.at[s], xs.at[s + 1], sh_send.at[s], sh_recv.at[s], r, d + 1).start()

        current = dot_rows(drive[...], inv[pl.ds(pl.multiple_of(r * P, P), P), :])
        for o in range(R - 1):
            remote(red_out.at[o], red_in.at[o], red_send.at[o], red_recv.at[o], r, d).wait()
            current = current + red_in[o].astype(F32)
        out[s] = current

        @pl.when(d == 0)
        def _():
            for e in (2, 1):
                remote(drive, drive, drv_send.at[e - 1], drv_recv, r, e).wait_send()

        @pl.when(d == 2)
        def _():
            remote(drive, drive, drv_send.at[0], drv_recv, r, 3).wait_send()

        if s < S - 1:
            mine = d * R + r
            newest[s] = current.astype(BF16)
            for o in list(range(1, Z)) + [0]:
                send = remote(newest.at[s], xs.at[s + 1, mine], pc_send.at[s, o],
                              pc_recv.at[s, mine], lane(o), 0)
                if o == 0:
                    pl.when(d != 0)(send.start)
                else:
                    send.start()

            @pl.when(d == 0)
            def _():
                xs[s + 1, mine] = current.astype(BF16)

    for s in range(S - 1):
        for o in range(Z):
            send = remote(newest.at[s], newest.at[s], pc_send.at[s, o], pc_recv.at[s, 0], r, 0)
            if o == 0:
                pl.when(d != 0)(send.wait_send)
            else:
                send.wait_send()

        @pl.when(d < D - 1)
        def _():
            if s == 0:
                for o in range(R):
                    shift_block(o).wait_send()
            else:
                remote(xs.at[s], xs.at[s + 1], sh_send.at[s], sh_recv.at[s], r, d + 1).wait_send()


def in_one_kernel(excitation, past_currents, history_mats, inverse):
    R, D = lax.axis_size("rows"), lax.axis_size("delay")
    S, E, W = excitation.shape
    N, P, Z = W * R, W // D, R // 2
    NP = R * D
    dma = pltpu.SemaphoreType.DMA
    vmem, anywhere = pl.BlockSpec(memory_space=pltpu.VMEM), pl.BlockSpec(memory_space=pl.ANY)
    return pl.pallas_call(
        functools.partial(march, R, D, S),
        out_shape=jax.ShapeDtypeStruct((S, E, P), F32),
        in_specs=[vmem, vmem, anywhere, anywhere],
        out_specs=vmem,
        scratch_shapes=[
            pltpu.VMEM((S, NP, E, P), BF16),
            pltpu.VMEM((SLOTS, W, P), BF16),
            pltpu.VMEM((N // D, W), BF16),
            pltpu.VMEM((E, W), F32),
            pltpu.VMEM((D - 1, E, W), BF16),
            pltpu.VMEM((E, W), BF16),
            pltpu.VMEM((E, W), BF16),
            pltpu.VMEM((R - 1, E, P), BF16),
            pltpu.VMEM((R - 1, E, P), BF16),
            pltpu.VMEM((S - 1, E, P), BF16),
            dma((SLOTS,)), dma(()),
            dma((Z - 1,)), dma((R,)), dma((Z,)),
            dma((S - 1, Z)), dma((S - 1, NP)), dma((Z * D,)),
            dma((S - 1,)), dma((S - 1,)), dma((R,)), dma((R,)),
            dma(()), dma((D - 1,)),
            dma((D - 1,)), dma(()),
            dma((R - 1,)), dma((R - 1,)),
        ],
        compiler_params=pltpu.CompilerParams(
            collective_id=0, has_side_effects=True, vmem_limit_bytes=62 * 2**20),
        cost_estimate=pl.CostEstimate(
            flops=2 * S * E * (N * W + N // D * W), bytes_accessed=2 * S * N * W, transcendentals=0),
    )(excitation, past_currents[0], history_mats[0], inverse)


def solution(mesh):
    in_specs = (
        P(None, None, "rows"),
        P("delay", None, "rows"),
        P("delay", "rows", None),
        P("delay", "rows"),
    )
    out_specs = P(None, None, ("delay", "rows"))
    rows, delays = mesh.shape["rows"], mesh.shape["delay"]

    def body(excitation, past_currents, history_mats, inverse):
        steps, _, width = excitation.shape
        fits = width % (delays * 128) == 0 and rows % 2 == 0 and rows <= 8 and delays == 4
        run = in_one_kernel if fits else on_device
        return run(excitation, past_currents, history_mats, inverse)

    return jax.shard_map(
        body, mesh=mesh, in_specs=in_specs, out_specs=out_specs, check_vma=False
    )
```
